32 devices in a mesh: img: 2 (over y), az: 8 (over z, x), rg: 2 (over core).
Axes of the slice: x: 2, y: 2, z: 4, core: 2. Of those that a mesh axis runs over, the one named last changes fastest.
Arguments:
- history: float32 [2, 2048, 2048], P(None, ('img', 'rg'), 'az'), parts along dimension 1, may hold values from -6 to 6
- coeffs: float32 [1024, 384], P('rg'), may hold values from -0.625 to 0.625
- band_width: int32 [1024], P('rg'), may hold values from 1 to 48, as said below
- block_shift: int32 [8], P('rg'), may hold values from -32 to 32, as said below
- scatter_rows: int32 [128], P('img'), parts along dimension 0, may hold values from 0 to 1023
- window_width: int32 [128], P('img'), parts along dimension 0, may hold values from 8 to 128, as said below
Outputs:
- spectrum: float32 [2, 2048, 2048], P(None, ('img', 'rg'), 'az'), parts along dimension 1
- phase: float32 [4096], P(('img', 'az')), parts along dimension 0
The draws below stay inside these ranges and needn't reach their ends.
There are 2 independent parts, one for each index of `img`. The reference program is written for one: setup_inputs(seed, part) draws one part's arguments, and reference() takes and returns one part's arrays. A program takes and returns all parts, laid end to end along the dimension named above; an argument that names none is the same for every part. Nothing has to cross between parts.
Inputs may be any that keep to these rules, and one draw needn't show every extreme that they name: `band_width`: the largest half-width 48 is taken by some row and the smallest, 1, by another. `block_shift`: offsets 32 and -32 both occur. `window_width`: Half-widths 128 and 8 both occur.
All inputs are finite; a program needn't handle non-finite values.
Results may differ from the reference program's by a relative error of at most 0.0003.
Values sent between devices are 32-bit elements; how exact they have to be, the bound alone decides.
A program may use at most 64 MiB of HBM per device.

```python
import jax
import jax.numpy as jnp
from jax import lax

A_DEV = 256
BLOCK = 128
WB = 48
OFF = 32
S = 64
NA = 2048
NR = 1024
W_MAX = 128


def draw_band_width(key, part):
    key = jax.random.fold_in(key, 11)
    widths = jax.random.randint(key, (NR,), 1, WB + 1, dtype=jnp.int32)
    return widths.at[0].set(WB).at[1].set(1)


def draw_block_shift(key, part):
    key = jax.random.fold_in(key, 12)
    count = NR // BLOCK
    value_key, first_key, second_key = jax.random.split(key, 3)
    shifts = jax.random.randint(value_key, (count,), 0 - OFF, OFF + 1, dtype=jnp.int32)
    first = jax.random.randint(first_key, (), 0, count, dtype=jnp.int32)
    second = (first + jax.random.randint(second_key, (), 1, count, dtype=jnp.int32)) % count
    return shifts.at[first].set(OFF).at[second].set(0 - OFF)


def draw_window_width(key, part):
    key = jax.random.fold_in(key, 13)
    widths = jax.random.randint(key, (S,), 8, W_MAX + 1, dtype=jnp.int32)
    return widths.at[0].set(W_MAX).at[1].set(8)


def place_ends(array, own_key, low, high):
    longest = array.shape.index(max(array.shape))
    spots = []
    for shift in (0, 1):
        where = [jax.random.randint(jax.random.fold_in(own_key, axis), (), 0, length) for axis, length in enumerate(array.shape)]
        where[longest] = (where[longest] + shift) % array.shape[longest]
        spots.append(tuple(where))
    return array.at[spots[0]].set(low).at[spots[1]].set(high)


def block_scale(key, shape, cuts, least, top_value):
    def one(axis_at, shards_of):
        heights = jax.random.uniform(jax.random.fold_in(jax.random.fold_in(key, 6), axis_at), (shards_of,), jnp.float32, least / len(cuts), top_value / len(cuts))
        return jnp.repeat(jnp.exp(heights), shape[axis_at] // shards_of).reshape((-1,) + (1,) * (len(shape) - axis_at - 1))

    gain = one(*cuts[0])
    for cut in cuts[1:]:
        gain = gain * one(*cut)
    return gain


def normal_values(rng, extent, width, bound, cuts=(), kind=jnp.bfloat16):
    array = width * jax.random.normal(rng, extent, jnp.float32)
    if cuts:
        array = array * block_scale(rng, extent, cuts, -0.22, 0.18)
    return jnp.clip(array, -bound, bound).astype(kind)


def setup_inputs(seed: int = 0, part: int = 0) -> dict:
    splits = jax.random.split(jax.random.key(seed), 7)
    part_splits = jax.random.split(jax.random.fold_in(splits[6], part), 7)
    return {
        "history": normal_values(part_splits[0], (2, NR, NA), 1.0, 6.0, ((1, 2), (2, 8)), jnp.float32),
        "coeffs": normal_values(splits[1], (NR, 3 * BLOCK), (2 * WB) ** -0.5, 0.625, ((0, 2),), jnp.float32),
        "band_width": draw_band_width(jax.random.fold_in(splits[6], 71), part),
        "block_shift": draw_block_shift(jax.random.fold_in(splits[6], 71), part),
        "scatter_rows": place_ends(jax.random.randint(part_splits[4], (S,), 0, NR), jax.random.fold_in(part_splits[4], 1), 0, NR - 1).astype(jnp.int32),
        "window_width": draw_window_width(jax.random.fold_in(jax.random.fold_in(splits[6], part), 71), part),
    }


def bit_flip(values, bits):
    flipped = jnp.zeros_like(values)
    for bit in range(bits):
        flipped = flipped | (((values >> bit) & 1) << (bits - 1 - bit))
    return flipped


def reference(history, coeffs, band_width, block_shift, scatter_rows, window_width):
    panels = NA // A_DEV
    sections = panels.bit_length() - 1
    rows = jnp.arange(NR, dtype=jnp.int32)
    blocks = rows // BLOCK
    offsets = jnp.arange(3 * BLOCK, dtype=jnp.int32)
    source = BLOCK * (blocks - 1)[:, None] + offsets[None, :]
    keep = jnp.abs(source - rows[:, None] - block_shift[blocks][:, None]) <= band_width[:, None]
    weights = jnp.where(keep, coeffs, jnp.zeros_like(coeffs)).reshape(NR // BLOCK, BLOCK, 3 * BLOCK)
    padded = jnp.pad(history, ((0, 0), (BLOCK, BLOCK), (0, 0)))

    def one_block(index):
        window = lax.dynamic_slice_in_dim(padded, (index * BLOCK).astype(jnp.int32), 3 * BLOCK, 1)
        return jnp.einsum("it,ctn->cin", weights[index], window, precision=lax.Precision.HIGHEST)

    resampled = lax.map(one_block, jnp.arange(NR // BLOCK, dtype=jnp.int32))
    resampled = jnp.transpose(resampled, (1, 0, 2, 3)).reshape(2, NR, NA)
    order = bit_flip(jnp.arange(panels, dtype=jnp.int32), sections)
    grouped = resampled.reshape(2, NR, panels, A_DEV)[:, :, order, :]
    samples = jnp.transpose(grouped, (0, 1, 3, 2)).reshape(2, NR, NA)
    transformed = jnp.fft.fft(samples[0] + 1j * samples[1], axis=-1)
    spectrum = jnp.stack([jnp.real(transformed), jnp.imag(transformed)]).astype(history.dtype)
    picked = spectrum[:, scatter_rows, :]
    freq = jnp.arange(NA, dtype=jnp.int32)
    distance = jnp.minimum(freq, NA - freq)
    inside = distance[None, :] <= window_width[:, None]
    windowed = jnp.where(inside[None], picked, jnp.zeros_like(picked))
    signal = jnp.fft.ifft(windowed[0] + 1j * windowed[1], axis=-1) * NA
    following = jnp.roll(signal, -1, axis=-1)
    numer = jnp.sum(jnp.imag(jnp.conj(signal) * following), axis=0)
    denom = jnp.sum(jnp.real(signal) ** 2 + jnp.imag(signal) ** 2, axis=0)
    grad = (numer / (denom + 1e-6)).astype(history.dtype)
    mean = jnp.sum(grad) / NA
    position = jnp.arange(NA, dtype=jnp.int32).astype(history.dtype)
    phase = jnp.cumsum(grad) - grad - position * mean
    return spectrum, phase
```

```python
import functools
import math

import jax
import jax.numpy as jnp
import ml_dtypes
import numpy as np
from jax import lax
from jax.experimental import pallas as pl
from jax.experimental.pallas import tpu as pltpu
from jax.sharding import PartitionSpec as P

BLOCK = 128
SUB = 64
MESH = pl.DeviceIdType.MESH
BF = jnp.bfloat16
F32 = jnp.float32


def split_np(table):
    table = table.astype(np.float32)
    hi = table.astype(ml_dtypes.bfloat16)
    lo = (table - hi.astype(np.float32)).astype(ml_dtypes.bfloat16)
    return hi, lo


def make_tables(panels, cols):
    sections = panels.bit_length() - 1
    total = panels * cols
    k = np.arange(cols, dtype=np.int64)
    kk = np.where(k < cols // 2, k, k - cols)
    ang = 2.0 * math.pi * (np.outer(k, k) % cols) / cols
    c, s = np.cos(ang), np.sin(ang)
    dft = split_np(np.block([[c, -s], [s, c]]))
    ang = 2.0 * math.pi * (np.outer(kk, k) % total) / total
    c, s = np.cos(ang), np.sin(ang)
    inv = split_np(np.block([[c, s], [-s, c]]))
    count = 4 + 4 * sections
    factors = np.zeros((panels, -(-count // 8) * 8, cols))
    for d in range(panels):
        rev = int(format(d, "b").zfill(sections)[::-1], 2)
        ang = -2.0 * math.pi * (rev * k % total) / total
        factors[d, 0], factors[d, 1] = np.cos(ang), np.sin(ang)
        ang = np.where(k < cols // 2, 0.0, 2.0 * math.pi * rev / panels)
        factors[d, 2], factors[d, 3] = np.cos(ang), np.sin(ang)
        for bit in range(sections):
            half = 1 << bit
            turn = np.exp(-1j * math.pi * (d % half) / half)
            own, other = (1.0, turn) if not d >> bit & 1 else (-turn, 1.0)
            at = 4 + 4 * bit
            factors[d, at], factors[d, at + 1] = np.real(own), np.imag(own)
            factors[d, at + 2], factors[d, at + 3] = np.real(other), np.imag(other)
    ang = 2.0 * math.pi * (np.outer(np.arange(panels), kk) % panels) / panels
    phases = np.concatenate([np.cos(ang), np.sin(ang)], axis=1)
    ang = 2.0 * math.pi * (cols // 2 * k % total) / total
    edge = np.concatenate([np.cos(ang), np.sin(ang)])[None, :]
    return dft + inv + (factors.astype(np.float32), phases.astype(np.float32), edge.astype(np.float32))


def split(value):
    hi = value.astype(BF)
    return hi, (value - hi.astype(F32)).astype(BF)


def dot(a, b):
    return jnp.dot(a, b, preferred_element_type=F32)


def dot3(a, bhi, blo):
    hi, lo = split(a)
    return dot(hi, bhi) + (dot(hi, blo) + dot(lo, bhi))


def kernel(
    panels, rows, cols, scat,
    shift_ref, hist_ref, coef_ref, aux_ref, dhi_ref, dlo_ref, ihi_ref, ilo_ref, fac_ref, ph_ref, edge_ref,
    out_ref, phase_ref,
    halo, xhi, xlo, st, rv, auxt, pick, grx, g1, g1rx, g2, g2rx, acc, sig, nd, ndrx,
    halo_send, halo_recv, send, recv, gsend, grecv,
):
    sections = panels.bit_length() - 1
    nblocks = rows // BLOCK
    subs = BLOCK // SUB
    chunks = nblocks * subs
    total = panels * cols
    az = lax.axis_index("az")
    rg = lax.axis_index("rg")
    core = {"rg": 1 - rg}
    peers = []
    for bit in range(sections):
        half = 1 << bit
        low = 1 - az // half % 2
        peers.append({"az": az + half * (2 * low - 1)})
    barrier = pltpu.get_barrier_semaphore()
    for peer in [core] + peers:
        pl.semaphore_signal(barrier, inc=1, device_id=peer, device_id_type=MESH)
    pl.semaphore_wait(barrier, sections + 1)

    def block_row(p):
        return pl.multiple_of(BLOCK * (p + rg * (nblocks - 1 - 2 * p)), BLOCK)

    halo_copy = pltpu.make_async_remote_copy(
        src_ref=hist_ref.at[:, pl.ds(block_row(nblocks - 1), BLOCK), :], dst_ref=halo,
        send_sem=halo_send, recv_sem=halo_recv, device_id=core, device_id_type=MESH,
    )
    halo_copy.start()

    def chunk_rows(chunk):
        return pl.ds(pl.multiple_of(block_row(chunk // subs) + SUB * (chunk % subs), SUB), SUB)

    def piece(bit, chunk):
        part = chunk_rows(chunk)
        return pltpu.make_async_remote_copy(
            src_ref=st.at[bit, part, :], dst_ref=rv.at[bit, part, :],
            send_sem=send.at[bit, chunk], recv_sem=recv.at[bit, chunk],
            device_id=peers[bit], device_id_type=MESH,
        )

    pieces = [[piece(bit, chunk) for chunk in range(chunks)] for bit in range(sections)]

    def put(at, value):
        hi, lo = split(value)
        xhi[at, :] = hi
        xlo[at, :] = lo

    for b in range(nblocks + 1):
        auxt[b] = jnp.broadcast_to(aux_ref[b : b + 1, :], (BLOCK, BLOCK)).T
    outer = pl.ds(pl.multiple_of(rg * (rows + BLOCK), BLOCK), BLOCK)
    xhi[outer, :] = jnp.zeros((BLOCK, 2 * cols), BF)
    xlo[outer, :] = jnp.zeros((BLOCK, 2 * cols), BF)

    def load(p):
        base = block_row(p)
        at = pl.ds(base + BLOCK, BLOCK)
        here = pl.ds(base, BLOCK)
        put(at, jnp.concatenate([hist_ref[0, here, :], hist_ref[1, here, :]], axis=1))

    def spin(value, cosine, sine):
        re, im = value[:, :cols], value[:, cols:]
        return re * cosine - im * sine, re * sine + im * cosine

    def factor(row):
        return fac_ref[az, row : row + 1, :]

    lane3 = lax.broadcasted_iota(jnp.int32, (BLOCK, 3 * BLOCK), 1)
    row3 = lax.broadcasted_iota(jnp.int32, (BLOCK, 3 * BLOCK), 0)

    def first(p):
        base = block_row(p)
        b = p + rg * (nblocks - 1 - 2 * p)
        width = auxt[b]
        width = jnp.concatenate([width, width, width], axis=1)
        keep = jnp.abs(lane3 - BLOCK - row3 - shift_ref[b]) <= width
        weight = jnp.where(keep, coef_ref[pl.ds(base, BLOCK), :], 0.0)
        window = pl.ds(base, 3 * BLOCK)
        value = dot3(weight, xhi[window, :], xlo[window, :])
        value = dot3(value, dhi_ref[...], dlo_ref[...])
        re, im = spin(value, factor(0), factor(1))
        st[0, pl.ds(base, BLOCK), :cols] = re
        st[0, pl.ds(base, BLOCK), cols:] = im
        for sub in range(subs):
            pieces[0][subs * p + sub].start()

    def merged(bit, chunk):
        part = chunk_rows(chunk)
        pieces[bit][chunk].wait_recv()
        at = 4 + 4 * bit
        re, im = spin(st[bit, part, :], factor(at), factor(at + 1))
        re2, im2 = spin(rv[bit, part, :], factor(at + 2), factor(at + 3))
        return part, re + re2, im + im2

    def advance(bit, chunk):
        part, re, im = merged(bit, chunk)
        st[bit + 1, part, :cols] = re
        st[bit + 1, part, cols:] = im
        pieces[bit + 1][chunk].start()

    def finish(chunk):
        part, re, im = merged(sections - 1, chunk)
        out_ref[0, part, :] = re
        out_ref[1, part, :] = im

    half = scat // 2
    quarter = scat // 4
    wide = 2 * cols + BLOCK
    low0 = 1 - az % 2

    def link(src, dst, slot, peer):
        return pltpu.make_async_remote_copy(
            src_ref=src, dst_ref=dst, send_sem=gsend.at[slot], recv_sem=grecv.at[slot],
            device_id=peer, device_id_type=MESH,
        )

    def half_at(side):
        return pl.ds(pl.multiple_of(side * half, half), half)

    def quarter_at(side):
        return pl.ds(pl.multiple_of(side * quarter, quarter), quarter)

    links = [
        link(pick.at[half_at(1 - rg), :], grx, 0, core),
        link(g1.at[quarter_at(low0), :], g1rx, 1, peers[0]),
    ]
    for bit in range(1, sections):
        links.append(link(g2.at[bit - 1], g2rx.at[bit - 1], 1 + bit, peers[bit]))
    links.append(link(nd.at[0], ndrx.at[0], sections + 1, peers[0]))
    links.append(link(nd.at[1], ndrx.at[1], sections + 2, core))

    def g_pick():
        where = auxt[nblocks, 0:scat, :]
        where = jnp.concatenate([where] * (rows // BLOCK), axis=1)
        index = lax.broadcasted_iota(jnp.int32, (scat, rows), 1) + rg * rows
        onehot = (where == index).astype(F32).astype(BF)
        hi, lo = split(st[0])
        value = dot(onehot, hi) + dot(onehot, lo)
        re, im = spin(value, factor(2), factor(3))
        pick[:, :cols] = re
        pick[:, cols : 2 * cols] = im
        lane = lax.broadcasted_iota(jnp.int32, (scat, BLOCK), 1)
        mid = cols // 2
        re_mid = value[:, mid : mid + BLOCK]
        im_mid = value[:, cols + mid : cols + mid + BLOCK]
        pick[:, 2 * cols :] = jnp.where(lane == 0, re_mid, pltpu.roll(im_mid, 1, 1))
        links[0].start()

    def g_core():
        links[0].wait_recv()
        g1[...] = pick[half_at(rg), :] + grx[...]
        links[1].start()

    def g_bit0():
        links[1].wait_recv()
        g2[0] = g1[quarter_at(1 - low0), :] + g1rx[...]
        if sections > 1:
            links[2].start()

    def g_bit(bit):
        links[1 + bit].wait_recv()
        g2[bit] = g2[bit - 1] + g2rx[bit - 1]
        if bit < sections - 1:
            links[2 + bit].start()

    lane_q = lax.broadcasted_iota(jnp.int32, (quarter, cols), 1)

    def g_signal():
        value = g2[sections - 1]
        mine = pl.multiple_of(scat + rg * half + (1 - low0) * quarter, quarter)
        width = auxt[nblocks, pl.ds(mine, quarter), :]
        dist = jnp.where(lane_q < cols // 2, lane_q, cols - lane_q)
        inside = dist <= jnp.concatenate([width] * (cols // BLOCK), axis=1)
        re = jnp.where(inside, value[:, :cols], 0.0)
        im = jnp.where(inside, value[:, cols : 2 * cols], 0.0)
        ends = jnp.where(width >= cols // 2, value[:, 2 * cols :], 0.0)
        end_re, end_im = ends[:, 0:1], ends[:, 1:2]
        ec, es = edge_ref[:, :cols], edge_ref[:, cols:]
        extra = jnp.concatenate([end_re * ec - end_im * es, end_re * es + end_im * ec], axis=1)

        def fill(q, carry):
            c, s = ph_ref[pl.ds(q, 1), :cols], ph_ref[pl.ds(q, 1), cols:]
            at = pl.ds(pl.multiple_of(q * quarter, quarter), quarter)
            acc[at, :cols] = re * c - im * s
            acc[at, cols:] = re * s + im * c
            return carry

        lax.fori_loop(0, panels, fill, 0)
        sig[...] = dot3(acc[...], ihi_ref[...], ilo_ref[...])

        def reduce(q, carry):
            at = pl.ds(pl.multiple_of(q * quarter, quarter), quarter)
            nxt = pl.ds(pl.multiple_of((q + 1) % panels * quarter, quarter), quarter)
            now = sig[at, :] + extra
            after = sig[nxt, :] + extra
            now_re, now_im = now[:, :cols], now[:, cols:]
            last = lane_q == cols - 1
            next_re = jnp.where(last, pltpu.roll(after[:, :cols], cols - 1, 1), pltpu.roll(now_re, cols - 1, 1))
            next_im = jnp.where(last, pltpu.roll(after[:, cols:], cols - 1, 1), pltpu.roll(now_im, cols - 1, 1))
            numer = jnp.sum(now_re * next_im - now_im * next_re, axis=0, keepdims=True)
            denom = jnp.sum(now_re * now_re + now_im * now_im, axis=0, keepdims=True)
            nd[0, pl.ds(q, 1), :cols] = numer
            nd[0, pl.ds(q, 1), cols:] = denom
            return carry

        lax.fori_loop(0, panels, reduce, 0)
        links[sections + 1].start()

    def g_sum0():
        links[sections + 1].wait_recv()
        nd[1] = nd[0] + ndrx[0]
        links[sections + 2].start()

    def g_phase():
        links[sections + 2].wait_recv()
        sums = nd[1] + ndrx[1]
        grad = sums[:, :cols] / (sums[:, cols:] + 1e-06)
        before = lax.broadcasted_iota(jnp.int32, (cols, cols), 0) < lax.broadcasted_iota(jnp.int32, (cols, cols), 1)
        tri = before.astype(F32)
        within = jnp.dot(grad, tri, precision=lax.Precision.HIGHEST, preferred_element_type=F32)
        totals = jnp.sum(grad, axis=1, keepdims=True)
        panel = lax.broadcasted_iota(jnp.int32, (panels, 1), 0)
        ahead = jnp.sum(jnp.where(panel < az, totals, 0.0), axis=0, keepdims=True)
        mean = jnp.sum(totals, axis=0, keepdims=True) / total
        own = lax.broadcasted_iota(jnp.int32, (panels, cols), 0) == az
        run = jnp.sum(jnp.where(own, within, 0.0), axis=0, keepdims=True)
        n = (az * cols + lax.broadcasted_iota(jnp.int32, (1, cols), 1)).astype(F32)
        phase_ref[...] = ahead + run - n * mean

    tail = [g_pick, g_core, g_bit0]
    tail += [functools.partial(g_bit, bit) for bit in range(1, sections)]
    tail += [g_signal, g_sum0, g_phase]

    def halo_in():
        halo_copy.wait_recv()
        inner = pl.ds(pl.multiple_of((1 - rg) * (rows + BLOCK), BLOCK), BLOCK)
        put(inner, jnp.concatenate([halo[0], halo[1]], axis=1))

    load(0)
    load(1)
    first(0)
    load(2)
    first(1)
    for p in range(3, nblocks):
        load(p)
    done = 2
    for step in range(chunks + sections - 2):
        if step and step % 2 == 0 and done < nblocks:
            if done == nblocks - 1:
                halo_in()
            first(done)
            done += 1
        elif done == nblocks and tail:
            tail.pop(0)()
        for bit in range(sections - 1):
            chunk = step - bit
            if 0 <= chunk < chunks:
                advance(bit, chunk)
    for chunk in range(chunks):
        finish(chunk)
        if tail:
            tail.pop(0)()
    for step in tail:
        step()
    halo_copy.wait_send()
    for line in pieces:
        for copy in line:
            copy.wait_send()
    for copy in links:
        copy.wait_send()


def shards(history, coeffs, band_width, block_shift, scatter_rows, window_width):
    rows, cols = history.shape[1], history.shape[2]
    panels = lax.axis_size("az")
    sections = panels.bit_length() - 1
    scat = scatter_rows.shape[0]
    nblocks = rows // BLOCK
    chunks = rows // SUB
    small = jnp.concatenate([scatter_rows, window_width]).reshape(1, 2 * scat)
    aux = jnp.concatenate([band_width.reshape(nblocks, BLOCK), small], axis=0)
    tables = [jnp.asarray(t) for t in make_tables(panels, cols)]
    quarter = scat // 4
    wide = 2 * cols + BLOCK
    vmem = pl.BlockSpec(memory_space=pltpu.VMEM)
    state, phase = pl.pallas_call(
        functools.partial(kernel, panels, rows, cols, scat),
        out_shape=(
            jax.ShapeDtypeStruct((2, rows, cols), F32),
            jax.ShapeDtypeStruct((1, cols), F32),
        ),
        in_specs=[pl.BlockSpec(memory_space=pltpu.SMEM)] + [vmem] * 10,
        out_specs=(vmem, vmem),
        scratch_shapes=[
            pltpu.VMEM((2, BLOCK, cols), F32),
            pltpu.VMEM((rows + 2 * BLOCK, 2 * cols), BF),
            pltpu.VMEM((rows + 2 * BLOCK, 2 * cols), BF),
            pltpu.VMEM((sections, rows, 2 * cols), F32),
            pltpu.VMEM((sections, rows, 2 * cols), F32),
            pltpu.VMEM((nblocks + 1, BLOCK, BLOCK), jnp.int32),
            pltpu.VMEM((scat, wide), F32),
            pltpu.VMEM((scat // 2, wide), F32),
            pltpu.VMEM((scat // 2, wide), F32),
            pltpu.VMEM((quarter, wide), F32),
            pltpu.VMEM((sections, quarter, wide), F32),
            pltpu.VMEM((sections, quarter, wide), F32),
            pltpu.VMEM((panels * quarter, 2 * cols), F32),
            pltpu.VMEM((panels * quarter, 2 * cols), F32),
            pltpu.VMEM((2, panels, 2 * cols), F32),
            pltpu.VMEM((2, panels, 2 * cols), F32),
            pltpu.SemaphoreType.DMA,
            pltpu.SemaphoreType.DMA,
            pltpu.SemaphoreType.DMA((sections, chunks)),
            pltpu.SemaphoreType.DMA((sections, chunks)),
            pltpu.SemaphoreType.DMA((sections + 3,)),
            pltpu.SemaphoreType.DMA((sections + 3,)),
        ],
        compiler_params=pltpu.CompilerParams(
            collective_id=0, has_side_effects=True, vmem_limit_bytes=48 * 1024 * 1024
        ),
    )(block_shift, history, coeffs, aux, *tables)
    return state, phase.reshape(cols)


def solution(mesh):
    in_specs = (P(None, ("img", "rg"), "az"), P("rg", None), P("rg"), P("rg"), P("img"), P("img"))
    out_specs = (P(None, ("img", "rg"), "az"), P(("img", "az")))
    return jax.shard_map(shards, mesh=mesh, in_specs=in_specs, out_specs=out_specs, check_vma=False)
```

```python
import functools
import math

import jax
import jax.numpy as jnp
import ml_dtypes
import numpy as np
from jax import lax
from jax.experimental import pallas as pl
from jax.experimental.pallas import tpu as pltpu
from jax.sharding import PartitionSpec as P

BLOCK = 128
SUB = 32
MESH = pl.DeviceIdType.MESH
BF = jnp.bfloat16
F32 = jnp.float32


def split_np(table):
    table = table.astype(np.float32)
    hi = table.astype(ml_dtypes.bfloat16)
    lo = (table - hi.astype(np.float32)).astype(ml_dtypes.bfloat16)
    return hi, lo


def make_tables(panels, cols):
    sections = panels.bit_length() - 1
    total = panels * cols
    k = np.arange(cols, dtype=np.int64)
    kk = np.where(k < cols // 2, k, k - cols)
    ang = 2.0 * math.pi * (np.outer(k, k) % cols) / cols
    c, s = np.cos(ang), np.sin(ang)
    dft = split_np(np.block([[c, -s], [s, c]]))
    ang = 2.0 * math.pi * (np.outer(kk, k) % total) / total
    c, s = np.cos(ang), np.sin(ang)
    inv = split_np(np.block([[c, s], [-s, c]]))
    count = 4 + 4 * sections
    factors = np.zeros((panels, -(-count // 8) * 8, cols))
    for d in range(panels):
        rev = int(format(d, "b").zfill(sections)[::-1], 2)
        ang = -2.0 * math.pi * (rev * k % total) / total
        factors[d, 0], factors[d, 1] = np.cos(ang), np.sin(ang)
        ang = np.where(k < cols // 2, 0.0, 2.0 * math.pi * rev / panels)
        factors[d, 2], factors[d, 3] = np.cos(ang), np.sin(ang)
        for bit in range(sections):
            half = 1 << bit
            turn = np.exp(-1j * math.pi * (d % half) / half)
            own, other = (1.0, turn) if not d >> bit & 1 else (-turn, 1.0)
            at = 4 + 4 * bit
            factors[d, at], factors[d, at + 1] = np.real(own), np.imag(own)
            factors[d, at + 2], factors[d, at + 3] = np.real(other), np.imag(other)
    ang = 2.0 * math.pi * (np.outer(np.arange(panels), kk) % panels) / panels
    phases = np.concatenate([np.cos(ang), np.sin(ang)], axis=1)
    ang = 2.0 * math.pi * (cols // 2 * k % total) / total
    edge = np.concatenate([np.cos(ang), np.sin(ang)])[None, :]
    return dft + inv + (factors.astype(np.float32), phases.astype(np.float32), edge.astype(np.float32))


def split(value):
    hi = value.astype(BF)
    return hi, (value - hi.astype(F32)).astype(BF)


def dot(a, b):
    return jnp.dot(a, b, preferred_element_type=F32)


def dot3(a, bhi, blo):
    hi, lo = split(a)
    return dot(hi, bhi) + (dot(hi, blo) + dot(lo, bhi))


def kernel(
    panels, rows, cols, scat,
    shift_ref, hist_ref, coef_hbm, band_hbm, scat_hbm, wind_hbm, dhi_hbm, dlo_hbm, ihi_hbm, ilo_hbm,
    fac_hbm, ph_hbm, edge_hbm,
    out_ref, phase_ref,
    hist, coef_ref, band, scat_v, wind_v, dhi_ref, dlo_ref, ihi_ref, ilo_ref, fac_ref, ph_ref, edge_ref, local, done_rows, out_sem,
    halo, xhi, xlo, st, rv, auxt, pick, grx, g1, g1rx, g2, g2rx, acc, sig, nd, ndrx,
    halo_send, halo_recv, send, recv, gsend, grecv,
):
    sections = panels.bit_length() - 1
    nblocks = rows // BLOCK
    subs = BLOCK // SUB
    chunks = nblocks * subs
    total = panels * cols
    az = lax.axis_index("az")
    rg = lax.axis_index("rg")
    core = {"rg": 1 - rg}
    peers = []
    for bit in range(sections):
        half = 1 << bit
        low = 1 - az // half % 2
        peers.append({"az": az + half * (2 * low - 1)})
    barrier = pltpu.get_barrier_semaphore()
    for peer in [core] + peers:
        pl.semaphore_signal(barrier, inc=1, device_id=peer, device_id_type=MESH)

    def block_row(p):
        return pl.multiple_of(BLOCK * (p + rg * (nblocks - 1 - 2 * p)), BLOCK)

    fetched = []

    def fetch(src, dst):
        copy = pltpu.make_async_copy(src, dst, local.at[len(fetched)])
        copy.start()
        fetched.append(copy)
        return copy

    hist_in, coef_in = [], []
    band_in = fetch(band_hbm, band)
    for p in range(nblocks):
        at = pl.ds(block_row(p), BLOCK)
        hist_in.append(fetch(hist_ref.at[:, at, :], hist.at[:, at, :]))
        if p == 1:
            coef_in.append(fetch(coef_hbm.at[pl.ds(block_row(0), BLOCK), :], coef_ref.at[pl.ds(block_row(0), BLOCK), :]))
            dft_in = [fetch(dhi_hbm, dhi_ref), fetch(dlo_hbm, dlo_ref), fetch(fac_hbm.at[az], fac_ref)]
    for p in range(1, nblocks):
        at = pl.ds(block_row(p), BLOCK)
        coef_in.append(fetch(coef_hbm.at[at, :], coef_ref.at[at, :]))
    late_in = [
        fetch(scat_hbm, scat_v), fetch(wind_hbm, wind_v), fetch(ihi_hbm, ihi_ref), fetch(ilo_hbm, ilo_ref),
        fetch(ph_hbm, ph_ref), fetch(edge_hbm, edge_ref),
    ]
    pl.semaphore_wait(barrier, sections + 1)

    halo_copy = pltpu.make_async_remote_copy(
        src_ref=hist_ref.at[:, pl.ds(block_row(nblocks - 1), BLOCK), :], dst_ref=halo,
        send_sem=halo_send, recv_sem=halo_recv, device_id=core, device_id_type=MESH,
    )
    halo_copy.start()

    def chunk_rows(chunk):
        return pl.ds(pl.multiple_of(block_row(chunk // subs) + SUB * (chunk % subs), SUB), SUB)

    def piece(bit, chunk):
        part = chunk_rows(chunk)
        return pltpu.make_async_remote_copy(
            src_ref=st.at[bit, part, :], dst_ref=rv.at[bit, part, :],
            send_sem=send.at[bit, chunk], recv_sem=recv.at[bit, chunk],
            device_id=peers[bit], device_id_type=MESH,
        )

    pieces = [[piece(bit, chunk) for chunk in range(chunks)] for bit in range(sections)]

    def put(at, value):
        hi, lo = split(value)
        xhi[at, :] = hi
        xlo[at, :] = lo

    band_in.wait()
    for b in range(nblocks):
        auxt[b] = jnp.broadcast_to(band[b : b + 1, :], (BLOCK, BLOCK)).T
    outer = pl.ds(pl.multiple_of(rg * (rows + BLOCK), BLOCK), BLOCK)
    xhi[outer, :] = jnp.zeros((BLOCK, 2 * cols), BF)
    xlo[outer, :] = jnp.zeros((BLOCK, 2 * cols), BF)

    def load(p):
        base = block_row(p)
        at = pl.ds(base + BLOCK, BLOCK)
        here = pl.ds(base, BLOCK)
        hist_in[p].wait()
        put(at, jnp.concatenate([hist[0, here, :], hist[1, here, :]], axis=1))

    def spin(value, cosine, sine):
        re, im = value[:, :cols], value[:, cols:]
        return re * cosine - im * sine, re * sine + im * cosine

    def factor(row):
        return fac_ref[row : row + 1, :]

    lane3 = lax.broadcasted_iota(jnp.int32, (BLOCK, 3 * BLOCK), 1)
    row3 = lax.broadcasted_iota(jnp.int32, (BLOCK, 3 * BLOCK), 0)

    def first(p):
        base = block_row(p)
        b = p + rg * (nblocks - 1 - 2 * p)
        coef_in[p].wait()
        if p == 0:
            for copy in dft_in:
                copy.wait()
        width = auxt[b]
        width = jnp.concatenate([width, width, width], axis=1)
        keep = jnp.abs(lane3 - BLOCK - row3 - shift_ref[b]) <= width
        weight = jnp.where(keep, coef_ref[pl.ds(base, BLOCK), :], 0.0)
        window = pl.ds(base, 3 * BLOCK)
        value = dot3(weight, xhi[window, :], xlo[window, :])
        value = dot3(value, dhi_ref[...], dlo_ref[...])
        re, im = spin(value, factor(0), factor(1))
        st[0, pl.ds(base, BLOCK), :cols] = re
        st[0, pl.ds(base, BLOCK), cols:] = im
        for sub in range(subs):
            pieces[0][subs * p + sub].start()

    def merged(bit, chunk):
        part = chunk_rows(chunk)
        pieces[bit][chunk].wait_recv()
        at = 4 + 4 * bit
        re, im = spin(st[bit, part, :], factor(at), factor(at + 1))
        re2, im2 = spin(rv[bit, part, :], factor(at + 2), factor(at + 3))
        return part, re + re2, im + im2

    def advance(bit, chunk):
        part, re, im = merged(bit, chunk)
        st[bit + 1, part, :cols] = re
        st[bit + 1, part, cols:] = im
        pieces[bit + 1][chunk].start()

    stores = []

    def finish(chunk):
        part, re, im = merged(sections - 1, chunk)
        done_rows[0, part, :] = re
        done_rows[1, part, :] = im
        copy = pltpu.make_async_copy(done_rows.at[:, part, :], out_ref.at[:, part, :], out_sem.at[chunk])
        copy.start()
        stores.append(copy)

    half = scat // 2
    quarter = scat // 4
    wide = 2 * cols + BLOCK
    low0 = 1 - az % 2

    def link(src, dst, slot, peer):
        return pltpu.make_async_remote_copy(
            src_ref=src, dst_ref=dst, send_sem=gsend.at[slot], recv_sem=grecv.at[slot],
            device_id=peer, device_id_type=MESH,
        )

    def half_at(side):
        return pl.ds(pl.multiple_of(side * half, half), half)

    def quarter_at(side):
        return pl.ds(pl.multiple_of(side * quarter, quarter), quarter)

    links = [
        link(pick.at[half_at(1 - rg), :], grx, 0, core),
        link(g1.at[quarter_at(low0), :], g1rx, 1, peers[0]),
    ]
    for bit in range(1, sections):
        links.append(link(g2.at[bit - 1], g2rx.at[bit - 1], 1 + bit, peers[bit]))
    links.append(link(nd.at[0], ndrx.at[0], sections + 1, peers[0]))
    links.append(link(nd.at[1], ndrx.at[1], sections + 2, core))

    def g_pick():
        for copy in late_in:
            copy.wait()
        small = jnp.concatenate([scat_v[...], wind_v[...]], axis=1)
        auxt[nblocks] = jnp.broadcast_to(small, (BLOCK, BLOCK)).T
        where = auxt[nblocks, 0:scat, :]
        where = jnp.concatenate([where] * (rows // BLOCK), axis=1)
        index = lax.broadcasted_iota(jnp.int32, (scat, rows), 1) + rg * rows
        onehot = (where == index).astype(F32).astype(BF)
        hi, lo = split(st[0])
        value = dot(onehot, hi) + dot(onehot, lo)
        re, im = spin(value, factor(2), factor(3))
        pick[:, :cols] = re
        pick[:, cols : 2 * cols] = im
        lane = lax.broadcasted_iota(jnp.int32, (scat, BLOCK), 1)
        mid = cols // 2
        re_mid = value[:, mid : mid + BLOCK]
        im_mid = value[:, cols + mid : cols + mid + BLOCK]
        pick[:, 2 * cols :] = jnp.where(lane == 0, re_mid, pltpu.roll(im_mid, 1, 1))
        links[0].start()

    def g_core():
        links[0].wait_recv()
        g1[...] = pick[half_at(rg), :] + grx[...]
        links[1].start()

    def g_bit0():
        links[1].wait_recv()
        g2[0] = g1[quarter_at(1 - low0), :] + g1rx[...]
        if sections > 1:
            links[2].start()

    def g_bit(bit):
        links[1 + bit].wait_recv()
        g2[bit] = g2[bit - 1] + g2rx[bit - 1]
        if bit < sections - 1:
            links[2 + bit].start()

    lane_q = lax.broadcasted_iota(jnp.int32, (quarter, cols), 1)

    def g_signal():
        value = g2[sections - 1]
        mine = pl.multiple_of(scat + rg * half + (1 - low0) * quarter, quarter)
        width = auxt[nblocks, pl.ds(mine, quarter), :]
        dist = jnp.where(lane_q < cols // 2, lane_q, cols - lane_q)
        inside = dist <= jnp.concatenate([width] * (cols // BLOCK), axis=1)
        re = jnp.where(inside, value[:, :cols], 0.0)
        im = jnp.where(inside, value[:, cols : 2 * cols], 0.0)
        ends = jnp.where(width >= cols // 2, value[:, 2 * cols :], 0.0)
        end_re, end_im = ends[:, 0:1], ends[:, 1:2]
        ec, es = edge_ref[:, :cols], edge_ref[:, cols:]
        extra = jnp.concatenate([end_re * ec - end_im * es, end_re * es + end_im * ec], axis=1)

        def fill(q, carry):
            c, s = ph_ref[pl.ds(q, 1), :cols], ph_ref[pl.ds(q, 1), cols:]
            at = pl.ds(pl.multiple_of(q * quarter, quarter), quarter)
            acc[at, :cols] = re * c - im * s
            acc[at, cols:] = re * s + im * c
            return carry

        lax.fori_loop(0, panels, fill, 0)
        sig[...] = dot3(acc[...], ihi_ref[...], ilo_ref[...])

        def reduce(q, carry):
            at = pl.ds(pl.multiple_of(q * quarter, quarter), quarter)
            nxt = pl.ds(pl.multiple_of((q + 1) % panels * quarter, quarter), quarter)
            now = sig[at, :] + extra
            after = sig[nxt, :] + extra
            now_re, now_im = now[:, :cols], now[:, cols:]
            last = lane_q == cols - 1
            next_re = jnp.where(last, pltpu.roll(after[:, :cols], cols - 1, 1), pltpu.roll(now_re, cols - 1, 1))
            next_im = jnp.where(last, pltpu.roll(after[:, cols:], cols - 1, 1), pltpu.roll(now_im, cols - 1, 1))
            numer = jnp.sum(now_re * next_im - now_im * next_re, axis=0, keepdims=True)
            denom = jnp.sum(now_re * now_re + now_im * now_im, axis=0, keepdims=True)
            nd[0, pl.ds(q, 1), :cols] = numer
            nd[0, pl.ds(q, 1), cols:] = denom
            return carry

        lax.fori_loop(0, panels, reduce, 0)
        links[sections + 1].start()

    def g_sum0():
        links[sections + 1].wait_recv()
        nd[1] = nd[0] + ndrx[0]
        links[sections + 2].start()

    def g_phase():
        links[sections + 2].wait_recv()
        sums = nd[1] + ndrx[1]
        grad = sums[:, :cols] / (sums[:, cols:] + 1e-06)
        before = lax.broadcasted_iota(jnp.int32, (cols, cols), 0) < lax.broadcasted_iota(jnp.int32, (cols, cols), 1)
        tri = before.astype(F32)
        within = jnp.dot(grad, tri, precision=lax.Precision.HIGHEST, preferred_element_type=F32)
        totals = jnp.sum(grad, axis=1, keepdims=True)
        panel = lax.broadcasted_iota(jnp.int32, (panels, 1), 0)
        ahead = jnp.sum(jnp.where(panel < az, totals, 0.0), axis=0, keepdims=True)
        mean = jnp.sum(totals, axis=0, keepdims=True) / total
        own = lax.broadcasted_iota(jnp.int32, (panels, cols), 0) == az
        run = jnp.sum(jnp.where(own, within, 0.0), axis=0, keepdims=True)
        n = (az * cols + lax.broadcasted_iota(jnp.int32, (1, cols), 1)).astype(F32)
        phase_ref[...] = ahead + run - n * mean

    tail = [g_pick, g_core, g_bit0]
    tail += [functools.partial(g_bit, bit) for bit in range(1, sections)]
    tail += [g_signal, g_sum0, g_phase]

    def halo_in():
        halo_copy.wait_recv()
        inner = pl.ds(pl.multiple_of((1 - rg) * (rows + BLOCK), BLOCK), BLOCK)
        put(inner, jnp.concatenate([halo[0], halo[1]], axis=1))

    load(0)
    load(1)
    first(0)
    load(2)
    first(1)
    for p in range(3, nblocks):
        load(p)
    done = 2
    for step in range(chunks + sections - 2):
        if step and step % subs == 0 and done < nblocks:
            if done == nblocks - 1:
                halo_in()
            first(done)
            done += 1
        elif done == nblocks and tail:
            tail.pop(0)()
        for bit in range(sections - 1):
            chunk = step - bit
            if 0 <= chunk < chunks:
                advance(bit, chunk)
    for chunk in range(chunks):
        finish(chunk)
        if tail:
            tail.pop(0)()
    for step in tail:
        step()
    for copy in stores:
        copy.wait()
    halo_copy.wait_send()
    for line in pieces:
        for copy in line:
            copy.wait_send()
    for copy in links:
        copy.wait_send()


def shards(history, coeffs, band_width, block_shift, scatter_rows, window_width):
    rows, cols = history.shape[1], history.shape[2]
    panels = lax.axis_size("az")
    sections = panels.bit_length() - 1
    scat = scatter_rows.shape[0]
    nblocks = rows // BLOCK
    chunks = rows // SUB
    tables = [jnp.asarray(t) for t in make_tables(panels, cols)]
    quarter = scat // 4
    wide = 2 * cols + BLOCK
    vmem = pl.BlockSpec(memory_space=pltpu.VMEM)
    state, phase = pl.pallas_call(
        functools.partial(kernel, panels, rows, cols, scat),
        out_shape=(
            jax.ShapeDtypeStruct((2, rows, cols), F32),
            jax.ShapeDtypeStruct((1, cols), F32),
        ),
        in_specs=[pl.BlockSpec(memory_space=pltpu.SMEM)] + [pl.BlockSpec(memory_space=pltpu.HBM)] * 12,
        out_specs=(pl.BlockSpec(memory_space=pltpu.HBM), vmem),
        scratch_shapes=[
            pltpu.VMEM((2, rows, cols), F32),
            pltpu.VMEM((rows, 3 * BLOCK), F32),
            pltpu.VMEM((nblocks, BLOCK), jnp.int32),
            pltpu.VMEM((1, scat), jnp.int32),
            pltpu.VMEM((1, scat), jnp.int32),
            pltpu.VMEM((2 * cols, 2 * cols), BF),
            pltpu.VMEM((2 * cols, 2 * cols), BF),
            pltpu.VMEM((2 * cols, 2 * cols), BF),
            pltpu.VMEM((2 * cols, 2 * cols), BF),
            pltpu.VMEM(tables[4].shape[1:], F32),
            pltpu.VMEM(tables[5].shape, F32),
            pltpu.VMEM(tables[6].shape, F32),
            pltpu.SemaphoreType.DMA((2 * nblocks + 10,)),
            pltpu.VMEM((2, rows, cols), F32),
            pltpu.SemaphoreType.DMA((chunks,)),
            pltpu.VMEM((2, BLOCK, cols), F32),
            pltpu.VMEM((rows + 2 * BLOCK, 2 * cols), BF),
            pltpu.VMEM((rows + 2 * BLOCK, 2 * cols), BF),
            pltpu.VMEM((sections, rows, 2 * cols), F32),
            pltpu.VMEM((sections, rows, 2 * cols), F32),
            pltpu.VMEM((nblocks + 1, BLOCK, BLOCK), jnp.int32),
            pltpu.VMEM((scat, wide), F32),
            pltpu.VMEM((scat // 2, wide), F32),
            pltpu.VMEM((scat // 2, wide), F32),
            pltpu.VMEM((quarter, wide), F32),
            pltpu.VMEM((sections, quarter, wide), F32),
            pltpu.VMEM((sections, quarter, wide), F32),
            pltpu.VMEM((panels * quarter, 2 * cols), F32),
            pltpu.VMEM((panels * quarter, 2 * cols), F32),
            pltpu.VMEM((2, panels, 2 * cols), F32),
            pltpu.VMEM((2, panels, 2 * cols), F32),
            pltpu.SemaphoreType.DMA,
            pltpu.SemaphoreType.DMA,
            pltpu.SemaphoreType.DMA((sections, chunks)),
            pltpu.SemaphoreType.DMA((sections, chunks)),
            pltpu.SemaphoreType.DMA((sections + 3,)),
            pltpu.SemaphoreType.DMA((sections + 3,)),
        ],
        compiler_params=pltpu.CompilerParams(
            collective_id=0, has_side_effects=True, vmem_limit_bytes=56 * 1024 * 1024
        ),
    )(
        block_shift, history, coeffs, band_width.reshape(nblocks, BLOCK),
        scatter_rows.reshape(1, scat), window_width.reshape(1, scat), *tables,
    )
    return state, phase.reshape(cols)


def solution(mesh):
    in_specs = (P(None, ("img", "rg"), "az"), P("rg", None), P("rg"), P("rg"), P("img"), P("img"))
    out_specs = (P(None, ("img", "rg"), "az"), P(("img", "az")))
    return jax.shard_map(shards, mesh=mesh, in_specs=in_specs, out_specs=out_specs, check_vma=False)
```

```python
import functools
import math

import jax
import jax.numpy as jnp
import ml_dtypes
import numpy as np
from jax import lax
from jax.experimental import pallas as pl
from jax.experimental.pallas import tpu as pltpu
from jax.sharding import PartitionSpec as P

BLOCK = 128
SUB = 32
AHEAD = 3
MESH = pl.DeviceIdType.MESH
BF = jnp.bfloat16
F32 = jnp.float32


def split_np(table):
    table = table.astype(np.float32)
    hi = table.astype(ml_dtypes.bfloat16)
    lo = (table - hi.astype(np.float32)).astype(ml_dtypes.bfloat16)
    return hi, lo


def make_tables(panels, cols):
    sections = panels.bit_length() - 1
    total = panels * cols
    k = np.arange(cols, dtype=np.int64)
    kk = np.where(k < cols // 2, k, k - cols)
    ang = 2.0 * math.pi * (np.outer(k, k) % cols) / cols
    c, s = np.cos(ang), np.sin(ang)
    dft = split_np(np.block([[c, -s], [s, c]]))
    ang = 2.0 * math.pi * (np.outer(kk, k) % total) / total
    c, s = np.cos(ang), np.sin(ang)
    inv = split_np(np.block([[c, s], [-s, c]]))
    count = 4 + 4 * sections
    factors = np.zeros((panels, -(-count // 8) * 8, cols))
    for d in range(panels):
        rev = int(format(d, "b").zfill(sections)[::-1], 2)
        ang = -2.0 * math.pi * (rev * k % total) / total
        factors[d, 0], factors[d, 1] = np.cos(ang), np.sin(ang)
        ang = np.where(k < cols // 2, 0.0, 2.0 * math.pi * rev / panels)
        factors[d, 2], factors[d, 3] = np.cos(ang), np.sin(ang)
        for bit in range(sections):
            half = 1 << bit
            turn = np.exp(-1j * math.pi * (d % half) / half)
            own, other = (1.0, turn) if not d >> bit & 1 else (-turn, 1.0)
            at = 4 + 4 * bit
            factors[d, at], factors[d, at + 1] = np.real(own), np.imag(own)
            factors[d, at + 2], factors[d, at + 3] = np.real(other), np.imag(other)
    ang = 2.0 * math.pi * (np.outer(np.arange(panels), kk) % panels) / panels
    phases = np.concatenate([np.cos(ang), np.sin(ang)], axis=1)
    ang = 2.0 * math.pi * (cols // 2 * k % total) / total
    edge = np.concatenate([np.cos(ang), np.sin(ang)])[None, :]
    return dft + inv + (factors.astype(np.float32), phases.astype(np.float32), edge.astype(np.float32))


def split(value):
    hi = value.astype(BF)
    return hi, (value - hi.astype(F32)).astype(BF)


def dot(a, b):
    return jnp.dot(a, b, preferred_element_type=F32)


def dot3(a, bhi, blo):
    hi, lo = split(a)
    return dot(hi, bhi) + (dot(hi, blo) + dot(lo, bhi))


def kernel(
    panels, rows, cols, scat,
    shift_ref, hist_ref, coef_hbm, band_hbm, scat_hbm, wind_hbm, dhi_hbm, dlo_hbm, ihi_hbm, ilo_hbm,
    fac_hbm, ph_hbm, edge_hbm,
    out_ref, phase_ref,
    hist, coef_ref, band, scat_v, wind_v, dhi_ref, dlo_ref, ihi_ref, ilo_ref, fac_ref, ph_ref, edge_ref, local,
    halo, xhi, xlo, st, rv, auxt, pick, grx, g1, g1rx, g2, g2rx, acc, sig, nd, ndrx,
    halo_send, halo_recv, send, recv, gsend, grecv,
):
    sections = panels.bit_length() - 1
    nblocks = rows // BLOCK
    subs = BLOCK // SUB
    chunks = nblocks * subs
    total = panels * cols
    az = lax.axis_index("az")
    rg = lax.axis_index("rg")
    core = {"rg": 1 - rg}
    peers = []
    for bit in range(sections):
        half = 1 << bit
        low = 1 - az // half % 2
        peers.append({"az": az + half * (2 * low - 1)})
    barrier = pltpu.get_barrier_semaphore()
    for peer in [core] + peers:
        pl.semaphore_signal(barrier, inc=1, device_id=peer, device_id_type=MESH)

    def block_row(p):
        return pl.multiple_of(BLOCK * (p + rg * (nblocks - 1 - 2 * p)), BLOCK)

    fetched = []

    def fetch(src, dst):
        copy = pltpu.make_async_copy(src, dst, local.at[len(fetched)])
        copy.start()
        fetched.append(copy)
        return copy

    hist_in, coef_in = [], []
    band_in = fetch(band_hbm, band)
    for p in range(nblocks):
        at = pl.ds(block_row(p), BLOCK)
        hist_in.append(fetch(hist_ref.at[:, at, :], hist.at[:, at, :]))
        if p == 1:
            coef_in.append(fetch(coef_hbm.at[pl.ds(block_row(0), BLOCK), :], coef_ref.at[pl.ds(block_row(0), BLOCK), :]))
            dft_in = [fetch(dhi_hbm, dhi_ref), fetch(dlo_hbm, dlo_ref), fetch(fac_hbm.at[az], fac_ref)]
    for p in range(1, nblocks):
        at = pl.ds(block_row(p), BLOCK)
        coef_in.append(fetch(coef_hbm.at[at, :], coef_ref.at[at, :]))
    late_in = [
        fetch(scat_hbm, scat_v), fetch(wind_hbm, wind_v), fetch(ihi_hbm, ihi_ref), fetch(ilo_hbm, ilo_ref),
        fetch(ph_hbm, ph_ref), fetch(edge_hbm, edge_ref),
    ]
    pl.semaphore_wait(barrier, sections + 1)

    halo_copy = pltpu.make_async_remote_copy(
        src_ref=hist_ref.at[:, pl.ds(block_row(nblocks - 1), BLOCK), :], dst_ref=halo,
        send_sem=halo_send, recv_sem=halo_recv, device_id=core, device_id_type=MESH,
    )
    halo_copy.start()

    def chunk_rows(chunk):
        return pl.ds(pl.multiple_of(block_row(chunk // subs) + SUB * (chunk % subs), SUB), SUB)

    def piece(bit, chunk):
        part = chunk_rows(chunk)
        return pltpu.make_async_remote_copy(
            src_ref=st.at[bit, part, :], dst_ref=rv.at[bit, part, :],
            send_sem=send.at[bit, chunk], recv_sem=recv.at[bit, chunk],
            device_id=peers[bit], device_id_type=MESH,
        )

    pieces = [[piece(bit, chunk) for chunk in range(chunks)] for bit in range(sections)]

    def put(at, value):
        hi, lo = split(value)
        xhi[at, :] = hi
        xlo[at, :] = lo

    band_in.wait()
    outer = pl.ds(pl.multiple_of(rg * (rows + BLOCK), BLOCK), BLOCK)
    xhi[outer, :] = jnp.zeros((BLOCK, 2 * cols), BF)
    xlo[outer, :] = jnp.zeros((BLOCK, 2 * cols), BF)

    def load(p):
        base = block_row(p)
        at = pl.ds(base + BLOCK, BLOCK)
        here = pl.ds(base, BLOCK)
        hist_in[p].wait()
        put(at, jnp.concatenate([hist[0, here, :], hist[1, here, :]], axis=1))

    def spin(value, cosine, sine):
        re, im = value[:, :cols], value[:, cols:]
        return re * cosine - im * sine, re * sine + im * cosine

    def factor(row):
        return fac_ref[row : row + 1, :]

    lane3 = lax.broadcasted_iota(jnp.int32, (BLOCK, 3 * BLOCK), 1)
    row3 = lax.broadcasted_iota(jnp.int32, (BLOCK, 3 * BLOCK), 0)

    def first(p):
        base = block_row(p)
        b = p + rg * (nblocks - 1 - 2 * p)
        coef_in[p].wait()
        if p == 0:
            for copy in dft_in:
                copy.wait()
        width = jnp.broadcast_to(band[pl.ds(b, 1), :], (BLOCK, BLOCK)).T
        width = jnp.concatenate([width, width, width], axis=1)
        keep = jnp.abs(lane3 - BLOCK - row3 - shift_ref[b]) <= width
        weight = jnp.where(keep, coef_ref[pl.ds(base, BLOCK), :], 0.0)
        window = pl.ds(base, 3 * BLOCK)
        value = dot3(weight, xhi[window, :], xlo[window, :])
        value = dot3(value, dhi_ref[...], dlo_ref[...])
        re, im = spin(value, factor(0), factor(1))
        st[0, pl.ds(base, BLOCK), :cols] = re
        st[0, pl.ds(base, BLOCK), cols:] = im
        ready[0] = subs * (p + 1)
        pump()

    ready, limit, sent = [0], [AHEAD], [0]

    def pump():
        while sent[0] < min(ready[0], limit[0]):
            pieces[0][sent[0]].start()
            sent[0] += 1

    def merged(bit, chunk):
        part = chunk_rows(chunk)
        pieces[bit][chunk].wait_recv()
        if bit == 0:
            limit[0] = chunk + 1 + AHEAD
            pump()
        at = 4 + 4 * bit
        re, im = spin(st[bit, part, :], factor(at), factor(at + 1))
        re2, im2 = spin(rv[bit, part, :], factor(at + 2), factor(at + 3))
        return part, re + re2, im + im2

    def advance(bit, chunk):
        part, re, im = merged(bit, chunk)
        st[bit + 1, part, :cols] = re
        st[bit + 1, part, cols:] = im
        pieces[bit + 1][chunk].start()

    def finish(chunk):
        part, re, im = merged(sections - 1, chunk)
        out_ref[0, part, :] = re
        out_ref[1, part, :] = im

    half = scat // 2
    quarter = scat // 4
    wide = 2 * cols + BLOCK
    low0 = 1 - az % 2

    def link(src, dst, slot, peer):
        return pltpu.make_async_remote_copy(
            src_ref=src, dst_ref=dst, send_sem=gsend.at[slot], recv_sem=grecv.at[slot],
            device_id=peer, device_id_type=MESH,
        )

    def half_at(side):
        return pl.ds(pl.multiple_of(side * half, half), half)

    def quarter_at(side):
        return pl.ds(pl.multiple_of(side * quarter, quarter), quarter)

    links = [
        link(pick.at[half_at(1 - rg), :], grx, 0, core),
        link(g1.at[quarter_at(low0), :], g1rx, 1, peers[0]),
    ]
    for bit in range(1, sections):
        links.append(link(g2.at[bit - 1], g2rx.at[bit - 1], 1 + bit, peers[bit]))
    links.append(link(nd.at[0], ndrx.at[0], sections + 1, peers[0]))
    links.append(link(nd.at[1], ndrx.at[1], sections + 2, core))

    def g_pick():
        for copy in late_in:
            copy.wait()
        small = jnp.concatenate([scat_v[...], wind_v[...]], axis=1)
        auxt[nblocks] = jnp.broadcast_to(small, (BLOCK, BLOCK)).T
        where = auxt[nblocks, 0:scat, :]
        where = jnp.concatenate([where] * (rows // BLOCK), axis=1)
        index = lax.broadcasted_iota(jnp.int32, (scat, rows), 1) + rg * rows
        onehot = (where == index).astype(F32).astype(BF)
        hi, lo = split(st[0])
        value = dot(onehot, hi) + dot(onehot, lo)
        re, im = spin(value, factor(2), factor(3))
        pick[:, :cols] = re
        pick[:, cols : 2 * cols] = im
        lane = lax.broadcasted_iota(jnp.int32, (scat, BLOCK), 1)
        mid = cols // 2
        re_mid = value[:, mid : mid + BLOCK]
        im_mid = value[:, cols + mid : cols + mid + BLOCK]
        pick[:, 2 * cols :] = jnp.where(lane == 0, re_mid, pltpu.roll(im_mid, 1, 1))
        links[0].start()

    def g_core():
        links[0].wait_recv()
        g1[...] = pick[half_at(rg), :] + grx[...]
        links[1].start()

    def g_bit0():
        links[1].wait_recv()
        g2[0] = g1[quarter_at(1 - low0), :] + g1rx[...]
        if sections > 1:
            links[2].start()

    def g_bit(bit):
        links[1 + bit].wait_recv()
        g2[bit] = g2[bit - 1] + g2rx[bit - 1]
        if bit < sections - 1:
            links[2 + bit].start()

    lane_q = lax.broadcasted_iota(jnp.int32, (quarter, cols), 1)

    def g_signal():
        value = g2[sections - 1]
        mine = pl.multiple_of(scat + rg * half + (1 - low0) * quarter, quarter)
        width = auxt[nblocks, pl.ds(mine, quarter), :]
        dist = jnp.where(lane_q < cols // 2, lane_q, cols - lane_q)
        inside = dist <= jnp.concatenate([width] * (cols // BLOCK), axis=1)
        re = jnp.where(inside, value[:, :cols], 0.0)
        im = jnp.where(inside, value[:, cols : 2 * cols], 0.0)
        ends = jnp.where(width >= cols // 2, value[:, 2 * cols :], 0.0)
        end_re, end_im = ends[:, 0:1], ends[:, 1:2]
        ec, es = edge_ref[:, :cols], edge_ref[:, cols:]
        extra = jnp.concatenate([end_re * ec - end_im * es, end_re * es + end_im * ec], axis=1)

        def fill(q, carry):
            c, s = ph_ref[pl.ds(q, 1), :cols], ph_ref[pl.ds(q, 1), cols:]
            at = pl.ds(pl.multiple_of(q * quarter, quarter), quarter)
            acc[at, :cols] = re * c - im * s
            acc[at, cols:] = re * s + im * c
            return carry

        lax.fori_loop(0, panels, fill, 0)
        sig[...] = dot3(acc[...], ihi_ref[...], ilo_ref[...])

        def reduce(q, carry):
            at = pl.ds(pl.multiple_of(q * quarter, quarter), quarter)
            nxt = pl.ds(pl.multiple_of((q + 1) % panels * quarter, quarter), quarter)
            now = sig[at, :] + extra
            after = sig[nxt, :] + extra
            now_re, now_im = now[:, :cols], now[:, cols:]
            last = lane_q == cols - 1
            next_re = jnp.where(last, pltpu.roll(after[:, :cols], cols - 1, 1), pltpu.roll(now_re, cols - 1, 1))
            next_im = jnp.where(last, pltpu.roll(after[:, cols:], cols - 1, 1), pltpu.roll(now_im, cols - 1, 1))
            numer = jnp.sum(now_re * next_im - now_im * next_re, axis=0, keepdims=True)
            denom = jnp.sum(now_re * now_re + now_im * now_im, axis=0, keepdims=True)
            nd[0, pl.ds(q, 1), :cols] = numer
            nd[0, pl.ds(q, 1), cols:] = denom
            return carry

        lax.fori_loop(0, panels, reduce, 0)
        links[sections + 1].start()

    def g_sum0():
        links[sections + 1].wait_recv()
        nd[1] = nd[0] + ndrx[0]
        links[sections + 2].start()

    def g_phase():
        links[sections + 2].wait_recv()
        sums = nd[1] + ndrx[1]
        grad = sums[:, :cols] / (sums[:, cols:] + 1e-06)
        before = lax.broadcasted_iota(jnp.int32, (cols, cols), 0) < lax.broadcasted_iota(jnp.int32, (cols, cols), 1)
        tri = before.astype(F32)
        within = jnp.dot(grad, tri, precision=lax.Precision.HIGHEST, preferred_element_type=F32)
        totals = jnp.sum(grad, axis=1, keepdims=True)
        panel = lax.broadcasted_iota(jnp.int32, (panels, 1), 0)
        ahead = jnp.sum(jnp.where(panel < az, totals, 0.0), axis=0, keepdims=True)
        mean = jnp.sum(totals, axis=0, keepdims=True) / total
        own = lax.broadcasted_iota(jnp.int32, (panels, cols), 0) == az
        run = jnp.sum(jnp.where(own, within, 0.0), axis=0, keepdims=True)
        n = (az * cols + lax.broadcasted_iota(jnp.int32, (1, cols), 1)).astype(F32)
        phase_ref[...] = ahead + run - n * mean

    tail = [g_pick, g_core, g_bit0]
    tail += [functools.partial(g_bit, bit) for bit in range(1, sections)]
    tail += [g_signal, g_sum0, g_phase]

    def halo_in():
        halo_copy.wait_recv()
        inner = pl.ds(pl.multiple_of((1 - rg) * (rows + BLOCK), BLOCK), BLOCK)
        put(inner, jnp.concatenate([halo[0], halo[1]], axis=1))

    load(0)
    load(1)
    first(0)
    done = 1
    for step in range(chunks + sections - 2):
        if step % 2 and done < nblocks:
            if done == nblocks - 1:
                halo_in()
            else:
                load(done + 1)
            first(done)
            done += 1
        elif done == nblocks and tail and (step % 2 or len(tail) > sections + 3):
            tail.pop(0)()
        for bit in range(sections - 1):
            chunk = step - bit
            if 0 <= chunk < chunks:
                advance(bit, chunk)
    for chunk in range(chunks):
        finish(chunk)
        if tail:
            tail.pop(0)()
    for step in tail:
        step()
    halo_copy.wait_send()
    for line in pieces:
        for copy in line:
            copy.wait_send()
    for copy in links:
        copy.wait_send()


def shards(history, coeffs, band_width, block_shift, scatter_rows, window_width):
    rows, cols = history.shape[1], history.shape[2]
    panels = lax.axis_size("az")
    sections = panels.bit_length() - 1
    scat = scatter_rows.shape[0]
    nblocks = rows // BLOCK
    chunks = rows // SUB
    tables = [jnp.asarray(t) for t in make_tables(panels, cols)]
    quarter = scat // 4
    wide = 2 * cols + BLOCK
    vmem = pl.BlockSpec(memory_space=pltpu.VMEM)
    state, phase = pl.pallas_call(
        functools.partial(kernel, panels, rows, cols, scat),
        out_shape=(
            pltpu.VMEM((2, rows, cols), F32),
            jax.ShapeDtypeStruct((1, cols), F32),
        ),
        in_specs=[pl.BlockSpec(memory_space=pltpu.SMEM)] + [pl.BlockSpec(memory_space=pltpu.HBM)] * 12,
        out_specs=(vmem, vmem),
        scratch_shapes=[
            pltpu.VMEM((2, rows, cols), F32),
            pltpu.VMEM((rows, 3 * BLOCK), F32),
            pltpu.VMEM((nblocks, BLOCK), jnp.int32),
            pltpu.VMEM((1, scat), jnp.int32),
            pltpu.VMEM((1, scat), jnp.int32),
            pltpu.VMEM((2 * cols, 2 * cols), BF),
            pltpu.VMEM((2 * cols, 2 * cols), BF),
            pltpu.VMEM((2 * cols, 2 * cols), BF),
            pltpu.VMEM((2 * cols, 2 * cols), BF),
            pltpu.VMEM(tables[4].shape[1:], F32),
            pltpu.VMEM(tables[5].shape, F32),
            pltpu.VMEM(tables[6].shape, F32),
            pltpu.SemaphoreType.DMA((2 * nblocks + 10,)),
            pltpu.VMEM((2, BLOCK, cols), F32),
            pltpu.VMEM((rows + 2 * BLOCK, 2 * cols), BF),
            pltpu.VMEM((rows + 2 * BLOCK, 2 * cols), BF),
            pltpu.VMEM((sections, rows, 2 * cols), F32),
            pltpu.VMEM((sections, rows, 2 * cols), F32),
            pltpu.VMEM((nblocks + 1, BLOCK, BLOCK), jnp.int32),
            pltpu.VMEM((scat, wide), F32),
            pltpu.VMEM((scat // 2, wide), F32),
            pltpu.VMEM((scat // 2, wide), F32),
            pltpu.VMEM((quarter, wide), F32),
            pltpu.VMEM((sections, quarter, wide), F32),
            pltpu.VMEM((sections, quarter, wide), F32),
            pltpu.VMEM((panels * quarter, 2 * cols), F32),
            pltpu.VMEM((panels * quarter, 2 * cols), F32),
            pltpu.VMEM((2, panels, 2 * cols), F32),
            pltpu.VMEM((2, panels, 2 * cols), F32),
            pltpu.SemaphoreType.DMA,
            pltpu.SemaphoreType.DMA,
            pltpu.SemaphoreType.DMA((sections, chunks)),
            pltpu.SemaphoreType.DMA((sections, chunks)),
            pltpu.SemaphoreType.DMA((sections + 3,)),
            pltpu.SemaphoreType.DMA((sections + 3,)),
        ],
        compiler_params=pltpu.CompilerParams(
            collective_id=0, has_side_effects=True, vmem_limit_bytes=56 * 1024 * 1024
        ),
    )(
        block_shift, history, coeffs, band_width.reshape(nblocks, BLOCK),
        scatter_rows.reshape(1, scat), window_width.reshape(1, scat), *tables,
    )
    return state, phase.reshape(cols)


def solution(mesh):
    in_specs = (P(None, ("img", "rg"), "az"), P("rg", None), P("rg"), P("rg"), P("img"), P("img"))
    out_specs = (P(None, ("img", "rg"), "az"), P(("img", "az")))
    return jax.shard_map(shards, mesh=mesh, in_specs=in_specs, out_specs=out_specs, check_vma=False)
```

```python
import functools
import math

import jax
import jax.numpy as jnp
import ml_dtypes
import numpy as np
from jax import lax
from jax.experimental import pallas as pl
from jax.experimental.pallas import tpu as pltpu
from jax.sharding import PartitionSpec as P

BLOCK = 128
SUB = 32
AHEAD = 3
MESH = pl.DeviceIdType.MESH
BF = jnp.bfloat16
F32 = jnp.float32


def split_np(table):
    table = table.astype(np.float32)
    hi = table.astype(ml_dtypes.bfloat16)
    lo = (table - hi.astype(np.float32)).astype(ml_dtypes.bfloat16)
    return hi, lo


def make_tables(panels, cols):
    sections = panels.bit_length() - 1
    total = panels * cols
    k = np.arange(cols, dtype=np.int64)
    kk = np.where(k < cols // 2, k, k - cols)
    ang = 2.0 * math.pi * (np.outer(k, k) % cols) / cols
    c, s = np.cos(ang), np.sin(ang)
    dft = split_np(np.block([[c, -s], [s, c]]))
    ang = 2.0 * math.pi * (np.outer(kk, k) % total) / total
    c, s = np.cos(ang), np.sin(ang)
    inv = split_np(np.block([[c, s], [-s, c]]))
    count = 4 + 4 * sections
    factors = np.zeros((panels, -(-count // 8) * 8, cols))
    for d in range(panels):
        rev = int(format(d, "b").zfill(sections)[::-1], 2)
        ang = -2.0 * math.pi * (rev * k % total) / total
        factors[d, 0], factors[d, 1] = np.cos(ang), np.sin(ang)
        ang = np.where(k < cols // 2, 0.0, 2.0 * math.pi * rev / panels)
        factors[d, 2], factors[d, 3] = np.cos(ang), np.sin(ang)
        for bit in range(sections):
            half = 1 << bit
            turn = np.exp(-1j * math.pi * (d % half) / half)
            own, other = (1.0, turn) if not d >> bit & 1 else (-turn, 1.0)
            at = 4 + 4 * bit
            factors[d, at], factors[d, at + 1] = np.real(own), np.imag(own)
            factors[d, at + 2], factors[d, at + 3] = np.real(other), np.imag(other)
    ang = 2.0 * math.pi * (np.outer(np.arange(panels), kk) % panels) / panels
    phases = np.concatenate([np.cos(ang), np.sin(ang)], axis=1)
    ang = 2.0 * math.pi * (cols // 2 * k % total) / total
    edge = np.concatenate([np.cos(ang), np.sin(ang)])[None, :]
    return dft + inv + (factors.astype(np.float32), phases.astype(np.float32), edge.astype(np.float32))


def split(value):
    hi = value.astype(BF)
    return hi, (value - hi.astype(F32)).astype(BF)


def dot(a, b):
    return jnp.dot(a, b, preferred_element_type=F32)


def dot3(a, bhi, blo):
    hi, lo = split(a)
    return dot(hi, bhi) + (dot(hi, blo) + dot(lo, bhi))


def kernel(
    panels, rows, cols, scat,
    shift_ref, hist_ref, coef_hbm, band_hbm, scat_hbm, wind_hbm, dhi_hbm, dlo_hbm, ihi_hbm, ilo_hbm,
    fac_hbm, ph_hbm, edge_hbm,
    out_ref, phase_ref,
    hist, coef_ref, band, scat_v, wind_v, dhi_ref, dlo_ref, ihi_ref, ilo_ref, fac_ref, ph_ref, edge_ref, local,
    halo, xhi, xlo, st, rv, auxt, pick, grx, g1, g1rx, g2, g2rx, acc, sig, nd, ndrx,
    halo_send, halo_recv, send, recv, gsend, grecv,
):
    sections = panels.bit_length() - 1
    nblocks = rows // BLOCK
    subs = BLOCK // SUB
    chunks = nblocks * subs
    total = panels * cols
    az = lax.axis_index("az")
    rg = lax.axis_index("rg")
    core = {"rg": 1 - rg}
    peers = []
    for bit in range(sections):
        half = 1 << bit
        low = 1 - az // half % 2
        peers.append({"az": az + half * (2 * low - 1)})
    barrier = pltpu.get_barrier_semaphore()
    for peer in [core] + peers:
        pl.semaphore_signal(barrier, inc=1, device_id=peer, device_id_type=MESH)

    def block_row(p):
        return pl.multiple_of(BLOCK * (p + rg * (nblocks - 1 - 2 * p)), BLOCK)

    fetched = []

    def fetch(src, dst):
        copy = pltpu.make_async_copy(src, dst, local.at[len(fetched)])
        copy.start()
        fetched.append(copy)
        return copy

    hist_in, coef_in = [], []
    band_in = fetch(band_hbm, band)
    for p in range(nblocks):
        at = pl.ds(block_row(p), BLOCK)
        hist_in.append(fetch(hist_ref.at[:, at, :], hist.at[:, at, :]))
        if p == 1:
            coef_in.append(fetch(coef_hbm.at[pl.ds(block_row(0), BLOCK), :], coef_ref.at[pl.ds(block_row(0), BLOCK), :]))
            dft_in = [fetch(dhi_hbm, dhi_ref), fetch(dlo_hbm, dlo_ref), fetch(fac_hbm.at[az], fac_ref)]
    for p in range(1, nblocks):
        at = pl.ds(block_row(p), BLOCK)
        coef_in.append(fetch(coef_hbm.at[at, :], coef_ref.at[at, :]))
    late_in = [
        fetch(scat_hbm, scat_v), fetch(wind_hbm, wind_v), fetch(ihi_hbm, ihi_ref), fetch(ilo_hbm, ilo_ref),
        fetch(ph_hbm, ph_ref), fetch(edge_hbm, edge_ref),
    ]
    pl.semaphore_wait(barrier, sections + 1)

    halo_copy = pltpu.make_async_remote_copy(
        src_ref=hist_ref.at[:, pl.ds(block_row(nblocks - 1), BLOCK), :], dst_ref=halo,
        send_sem=halo_send, recv_sem=halo_recv, device_id=core, device_id_type=MESH,
    )
    halo_copy.start()

    def chunk_rows(chunk):
        return pl.ds(pl.multiple_of(block_row(chunk // subs) + SUB * (chunk % subs), SUB), SUB)

    def piece(bit, chunk):
        part = chunk_rows(chunk)
        return pltpu.make_async_remote_copy(
            src_ref=st.at[bit, part, :], dst_ref=rv.at[bit, part, :],
            send_sem=send.at[bit, chunk], recv_sem=recv.at[bit, chunk],
            device_id=peers[bit], device_id_type=MESH,
        )

    pieces = [[piece(bit, chunk) for chunk in range(chunks)] for bit in range(sections)]

    def put(at, value):
        hi, lo = split(value)
        xhi[at, :] = hi
        xlo[at, :] = lo

    band_in.wait()
    outer = pl.ds(pl.multiple_of(rg * (rows + BLOCK), BLOCK), BLOCK)
    xhi[outer, :] = jnp.zeros((BLOCK, 2 * cols), BF)
    xlo[outer, :] = jnp.zeros((BLOCK, 2 * cols), BF)

    def load(p):
        base = block_row(p)
        at = pl.ds(base + BLOCK, BLOCK)
        here = pl.ds(base, BLOCK)
        hist_in[p].wait()
        put(at, jnp.concatenate([hist[0, here, :], hist[1, here, :]], axis=1))

    def spin(value, cosine, sine):
        re, im = value[:, :cols], value[:, cols:]
        return re * cosine - im * sine, re * sine + im * cosine

    def factor(row):
        return fac_ref[row : row + 1, :]

    lane3 = lax.broadcasted_iota(jnp.int32, (BLOCK, 3 * BLOCK), 1)
    row3 = lax.broadcasted_iota(jnp.int32, (BLOCK, 3 * BLOCK), 0)

    def first(p):
        base = block_row(p)
        b = p + rg * (nblocks - 1 - 2 * p)
        coef_in[p].wait()
        if p == 0:
            for copy in dft_in:
                copy.wait()
        width = jnp.broadcast_to(band[pl.ds(b, 1), :], (BLOCK, BLOCK)).T
        width = jnp.concatenate([width, width, width], axis=1)
        keep = jnp.abs(lane3 - BLOCK - row3 - shift_ref[b]) <= width
        weight = jnp.where(keep, coef_ref[pl.ds(base, BLOCK), :], 0.0)
        window = pl.ds(base, 3 * BLOCK)
        size = BLOCK // 2 if p == 0 else BLOCK
        for top in range(0, BLOCK, size):
            value = dot3(weight[top : top + size], xhi[window, :], xlo[window, :])
            value = dot3(value, dhi_ref[...], dlo_ref[...])
            re, im = spin(value, factor(0), factor(1))
            st[0, pl.ds(base + top, size), :cols] = re
            st[0, pl.ds(base + top, size), cols:] = im
            ready[0] += size // SUB
            pump()

    ready, limit, sent = [0], [AHEAD], [0]

    def pump():
        while sent[0] < min(ready[0], limit[0]):
            pieces[0][sent[0]].start()
            sent[0] += 1

    def merged(bit, chunk):
        part = chunk_rows(chunk)
        pieces[bit][chunk].wait_recv()
        if bit == 0:
            limit[0] = chunk + 1 + AHEAD
            pump()
        at = 4 + 4 * bit
        re, im = spin(st[bit, part, :], factor(at), factor(at + 1))
        re2, im2 = spin(rv[bit, part, :], factor(at + 2), factor(at + 3))
        return part, re + re2, im + im2

    def advance(bit, chunk):
        part, re, im = merged(bit, chunk)
        st[bit + 1, part, :cols] = re
        st[bit + 1, part, cols:] = im
        pieces[bit + 1][chunk].start()

    def finish(chunk):
        part, re, im = merged(sections - 1, chunk)
        out_ref[0, part, :] = re
        out_ref[1, part, :] = im

    half = scat // 2
    quarter = scat // 4
    wide = 2 * cols + BLOCK
    low0 = 1 - az % 2

    def link(src, dst, slot, peer):
        return pltpu.make_async_remote_copy(
            src_ref=src, dst_ref=dst, send_sem=gsend.at[slot], recv_sem=grecv.at[slot],
            device_id=peer, device_id_type=MESH,
        )

    def half_at(side):
        return pl.ds(pl.multiple_of(side * half, half), half)

    def quarter_at(side):
        return pl.ds(pl.multiple_of(side * quarter, quarter), quarter)

    links = [
        link(pick.at[half_at(1 - rg), :], grx, 0, core),
        link(g1.at[quarter_at(low0), :], g1rx, 1, peers[0]),
    ]
    for bit in range(1, sections):
        links.append(link(g2.at[bit - 1], g2rx.at[bit - 1], 1 + bit, peers[bit]))
    links.append(link(nd.at[0], ndrx.at[0], sections + 1, peers[0]))
    links.append(link(nd.at[1], ndrx.at[1], sections + 2, core))

    def g_pick():
        for copy in late_in:
            copy.wait()
        small = jnp.concatenate([scat_v[...], wind_v[...]], axis=1)
        auxt[nblocks] = jnp.broadcast_to(small, (BLOCK, BLOCK)).T
        where = auxt[nblocks, 0:scat, :]
        where = jnp.concatenate([where] * (rows // BLOCK), axis=1)
        index = lax.broadcasted_iota(jnp.int32, (scat, rows), 1) + rg * rows
        onehot = (where == index).astype(F32).astype(BF)
        hi, lo = split(st[0])
        value = dot(onehot, hi) + dot(onehot, lo)
        re, im = spin(value, factor(2), factor(3))
        pick[:, :cols] = re
        pick[:, cols : 2 * cols] = im
        lane = lax.broadcasted_iota(jnp.int32, (scat, BLOCK), 1)
        mid = cols // 2
        re_mid = value[:, mid : mid + BLOCK]
        im_mid = value[:, cols + mid : cols + mid + BLOCK]
        pick[:, 2 * cols :] = jnp.where(lane == 0, re_mid, pltpu.roll(im_mid, 1, 1))
        links[0].start()

    def g_core():
        links[0].wait_recv()
        g1[...] = pick[half_at(rg), :] + grx[...]
        links[1].start()

    def g_bit0():
        links[1].wait_recv()
        g2[0] = g1[quarter_at(1 - low0), :] + g1rx[...]
        if sections > 1:
            links[2].start()

    def g_bit(bit):
        links[1 + bit].wait_recv()
        g2[bit] = g2[bit - 1] + g2rx[bit - 1]
        if bit < sections - 1:
            links[2 + bit].start()

    lane_q = lax.broadcasted_iota(jnp.int32, (quarter, cols), 1)

    def g_signal():
        value = g2[sections - 1]
        mine = pl.multiple_of(scat + rg * half + (1 - low0) * quarter, quarter)
        width = auxt[nblocks, pl.ds(mine, quarter), :]
        dist = jnp.where(lane_q < cols // 2, lane_q, cols - lane_q)
        inside = dist <= jnp.concatenate([width] * (cols // BLOCK), axis=1)
        re = jnp.where(inside, value[:, :cols], 0.0)
        im = jnp.where(inside, value[:, cols : 2 * cols], 0.0)
        ends = jnp.where(width >= cols // 2, value[:, 2 * cols :], 0.0)
        end_re, end_im = ends[:, 0:1], ends[:, 1:2]
        ec, es = edge_ref[:, :cols], edge_ref[:, cols:]
        extra = jnp.concatenate([end_re * ec - end_im * es, end_re * es + end_im * ec], axis=1)

        def fill(q, carry):
            c, s = ph_ref[pl.ds(q, 1), :cols], ph_ref[pl.ds(q, 1), cols:]
            at = pl.ds(pl.multiple_of(q * quarter, quarter), quarter)
            acc[at, :cols] = re * c - im * s
            acc[at, cols:] = re * s + im * c
            return carry

        lax.fori_loop(0, panels, fill, 0)
        sig[...] = dot3(acc[...], ihi_ref[...], ilo_ref[...])

        def reduce(q, carry):
            at = pl.ds(pl.multiple_of(q * quarter, quarter), quarter)
            nxt = pl.ds(pl.multiple_of((q + 1) % panels * quarter, quarter), quarter)
            now = sig[at, :] + extra
            after = sig[nxt, :] + extra
            now_re, now_im = now[:, :cols], now[:, cols:]
            last = lane_q == cols - 1
            next_re = jnp.where(last, pltpu.roll(after[:, :cols], cols - 1, 1), pltpu.roll(now_re, cols - 1, 1))
            next_im = jnp.where(last, pltpu.roll(after[:, cols:], cols - 1, 1), pltpu.roll(now_im, cols - 1, 1))
            numer = jnp.sum(now_re * next_im - now_im * next_re, axis=0, keepdims=True)
            denom = jnp.sum(now_re * now_re + now_im * now_im, axis=0, keepdims=True)
            nd[0, pl.ds(q, 1), :cols] = numer
            nd[0, pl.ds(q, 1), cols:] = denom
            return carry

        lax.fori_loop(0, panels, reduce, 0)
        links[sections + 1].start()

    def g_sum0():
        links[sections + 1].wait_recv()
        nd[1] = nd[0] + ndrx[0]
        links[sections + 2].start()

    def g_phase():
        links[sections + 2].wait_recv()
        sums = nd[1] + ndrx[1]
        grad = sums[:, :cols] / (sums[:, cols:] + 1e-06)
        before = lax.broadcasted_iota(jnp.int32, (cols, cols), 0) < lax.broadcasted_iota(jnp.int32, (cols, cols), 1)
        tri = before.astype(F32)
        within = jnp.dot(grad, tri, precision=lax.Precision.HIGHEST, preferred_element_type=F32)
        totals = jnp.sum(grad, axis=1, keepdims=True)
        panel = lax.broadcasted_iota(jnp.int32, (panels, 1), 0)
        ahead = jnp.sum(jnp.where(panel < az, totals, 0.0), axis=0, keepdims=True)
        mean = jnp.sum(totals, axis=0, keepdims=True) / total
        own = lax.broadcasted_iota(jnp.int32, (panels, cols), 0) == az
        run = jnp.sum(jnp.where(own, within, 0.0), axis=0, keepdims=True)
        n = (az * cols + lax.broadcasted_iota(jnp.int32, (1, cols), 1)).astype(F32)
        phase_ref[...] = ahead + run - n * mean

    tail = [g_pick, g_core, g_bit0]
    tail += [functools.partial(g_bit, bit) for bit in range(1, sections)]
    tail += [g_signal, g_sum0, g_phase]

    def halo_in():
        halo_copy.wait_recv()
        inner = pl.ds(pl.multiple_of((1 - rg) * (rows + BLOCK), BLOCK), BLOCK)
        put(inner, jnp.concatenate([halo[0], halo[1]], axis=1))

    load(0)
    load(1)
    first(0)
    done = 1
    for step in range(chunks + sections - 2):
        if step % 2 and done < nblocks:
            if done == nblocks - 1:
                halo_in()
            else:
                load(done + 1)
            first(done)
            done += 1
        elif done == nblocks and tail and (step % 2 or len(tail) > sections + 3):
            tail.pop(0)()
        for bit in range(sections - 1):
            chunk = step - bit
            if 0 <= chunk < chunks:
                advance(bit, chunk)
    for chunk in range(chunks):
        finish(chunk)
        if tail:
            tail.pop(0)()
    for step in tail:
        step()
    halo_copy.wait_send()
    for line in pieces:
        for copy in line:
            copy.wait_send()
    for copy in links:
        copy.wait_send()


def shards(history, coeffs, band_width, block_shift, scatter_rows, window_width):
    rows, cols = history.shape[1], history.shape[2]
    panels = lax.axis_size("az")
    sections = panels.bit_length() - 1
    scat = scatter_rows.shape[0]
    nblocks = rows // BLOCK
    chunks = rows // SUB
    tables = [jnp.asarray(t) for t in make_tables(panels, cols)]
    quarter = scat // 4
    wide = 2 * cols + BLOCK
    vmem = pl.BlockSpec(memory_space=pltpu.VMEM)
    state, phase = pl.pallas_call(
        functools.partial(kernel, panels, rows, cols, scat),
        out_shape=(
            pltpu.VMEM((2, rows, cols), F32),
            jax.ShapeDtypeStruct((1, cols), F32),
        ),
        in_specs=[pl.BlockSpec(memory_space=pltpu.SMEM)] + [pl.BlockSpec(memory_space=pltpu.HBM)] * 12,
        out_specs=(vmem, vmem),
        scratch_shapes=[
            pltpu.VMEM((2, rows, cols), F32),
            pltpu.VMEM((rows, 3 * BLOCK), F32),
            pltpu.VMEM((nblocks, BLOCK), jnp.int32),
            pltpu.VMEM((1, scat), jnp.int32),
            pltpu.VMEM((1, scat), jnp.int32),
            pltpu.VMEM((2 * cols, 2 * cols), BF),
            pltpu.VMEM((2 * cols, 2 * cols), BF),
            pltpu.VMEM((2 * cols, 2 * cols), BF),
            pltpu.VMEM((2 * cols, 2 * cols), BF),
            pltpu.VMEM(tables[4].shape[1:], F32),
            pltpu.VMEM(tables[5].shape, F32),
            pltpu.VMEM(tables[6].shape, F32),
            pltpu.SemaphoreType.DMA((2 * nblocks + 10,)),
            pltpu.VMEM((2, BLOCK, cols), F32),
            pltpu.VMEM((rows + 2 * BLOCK, 2 * cols), BF),
            pltpu.VMEM((rows + 2 * BLOCK, 2 * cols), BF),
            pltpu.VMEM((sections, rows, 2 * cols), F32),
            pltpu.VMEM((sections, rows, 2 * cols), F32),
            pltpu.VMEM((nblocks + 1, BLOCK, BLOCK), jnp.int32),
            pltpu.VMEM((scat, wide), F32),
            pltpu.VMEM((scat // 2, wide), F32),
            pltpu.VMEM((scat // 2, wide), F32),
            pltpu.VMEM((quarter, wide), F32),
            pltpu.VMEM((sections, quarter, wide), F32),
            pltpu.VMEM((sections, quarter, wide), F32),
            pltpu.VMEM((panels * quarter, 2 * cols), F32),
            pltpu.VMEM((panels * quarter, 2 * cols), F32),
            pltpu.VMEM((2, panels, 2 * cols), F32),
            pltpu.VMEM((2, panels, 2 * cols), F32),
            pltpu.SemaphoreType.DMA,
            pltpu.SemaphoreType.DMA,
            pltpu.SemaphoreType.DMA((sections, chunks)),
            pltpu.SemaphoreType.DMA((sections, chunks)),
            pltpu.SemaphoreType.DMA((sections + 3,)),
            pltpu.SemaphoreType.DMA((sections + 3,)),
        ],
        compiler_params=pltpu.CompilerParams(
            collective_id=0, has_side_effects=True, vmem_limit_bytes=56 * 1024 * 1024
        ),
    )(
        block_shift, history, coeffs, band_width.reshape(nblocks, BLOCK),
        scatter_rows.reshape(1, scat), window_width.reshape(1, scat), *tables,
    )
    return state, phase.reshape(cols)


def solution(mesh):
    in_specs = (P(None, ("img", "rg"), "az"), P("rg", None), P("rg"), P("rg"), P("img"), P("img"))
    out_specs = (P(None, ("img", "rg"), "az"), P(("img", "az")))
    return jax.shard_map(shards, mesh=mesh, in_specs=in_specs, out_specs=out_specs, check_vma=False)
```
